32 devices in a mesh: section: 4 (over y, x), rows: 8 (over z, core).
Axes of the slice: x: 2, y: 2, z: 4, core: 2. Of those that a mesh axis runs over, the one named last changes fastest.
Arguments:
- latents: bfloat16 [4, 8, 4, 640], P(None, None, None, 'rows'), may hold values from -20 to 20
- w_in: bfloat16 [3, 4, 512], replicated, may hold values from -1.75 to 1.75
- w_time: bfloat16 [3, 512, 512], replicated, may hold values from -0.15625 to 0.15625
- w_first: bfloat16 [3, 3, 512, 512], P(None, None, None, 'section'), may hold values from -0.09375 to 0.09375
- w_second: bfloat16 [3, 3, 512, 512], P(None, None, None, 'section'), may hold values from -0.09375 to 0.09375
Outputs:
- decoded: bfloat16 [128, 4, 160, 512], P('rows', None, None, 'section')
The draws below stay inside these ranges and needn't reach their ends.
All inputs are finite; a program needn't handle non-finite values.
Results may differ from the reference program's by a relative error of at most 0.0064.
Values may be sent and summed in bfloat16 or wider, within the bound.
A program may use at most 128 MiB of HBM per device.

```python
import math
import jax
import jax.numpy as jnp
from jax import lax

CH = 512
LATC = 4
GROUPS = 32
HS = 4
W = 160
CLIPS = 4
LF = 8
UPS = 4
FR = 32
FRAMES = 128
POS = 640


def draw_latents(key, part):
    key_base, key_rows, key_cols = jax.random.split(key, 3)
    base = jax.random.truncated_normal(key_base, -4.0, 4.0, (CLIPS, LF, LATC, HS, W), jnp.float32)
    row_scale = jnp.exp(jax.random.uniform(key_rows, (CLIPS, LF, 1, HS, 1), jnp.float32, math.log(0.3), math.log(3.0)))
    col_scale = jnp.exp(jax.random.uniform(key_cols, (1, 1, 1, 1, W), jnp.float32, math.log(0.5), math.log(1.6)))
    return (base * row_scale * col_scale).reshape(CLIPS, LF, LATC, HS * W).astype(jnp.bfloat16)


def block_scale(rng, extent, pieces, low, high):
    loudness = 1.0
    for dim, blocks in pieces:
        heights = jax.random.uniform(jax.random.fold_in(jax.random.fold_in(rng, 6), dim), (blocks,), jnp.float32, low / len(pieces), high / len(pieces))
        loudness = loudness * jnp.repeat(jnp.exp(heights), extent[dim] // blocks).reshape((-1,) + (1,) * (len(extent) - 1 - dim))
    return loudness


def scatter_about(rng, shape, spread, most, cuts=(), kind=jnp.bfloat16):
    entries = jax.random.normal(rng, shape, jnp.float32) * spread
    if len(cuts) > 0:
        entries = block_scale(rng, shape, cuts, -0.22, 0.18) * entries
    return jnp.clip(entries, min=-most, max=most).astype(kind)


def setup_inputs(seed: int = 0) -> dict:
    seeds = jax.random.split(jax.random.key(seed), 6)
    return {
        "latents": draw_latents(jax.random.fold_in(seeds[5], 71), 0),
        "w_in": scatter_about(seeds[1], (3, LATC, CH), (3 * LATC) ** -0.5, 1.75),
        "w_time": scatter_about(seeds[2], (3, CH, CH), (3 * CH) ** -0.5, 0.15625),
        "w_first": scatter_about(seeds[3], (3, 3, CH, CH), (9 * CH) ** -0.5, 0.09375, ((3, 4),)),
        "w_second": scatter_about(seeds[4], (3, 3, CH, CH), (9 * CH) ** -0.5, 0.09375, ((3, 4),)),
    }


def causal_taps(length, offset):
    return jnp.maximum(jnp.arange(length) - 2 + offset, 0)

def group_norm(values):
    frames, height, width, channels = values.shape
    grouped = values.reshape(frames, height, width, GROUPS, channels // GROUPS)
    mean = lax.optimization_barrier(jnp.mean(grouped, axis=(1, 2, 4), keepdims=True))
    centered = grouped - mean
    variance = lax.optimization_barrier(jnp.mean(centered * centered, axis=(1, 2, 4), keepdims=True))
    return (centered * lax.rsqrt(variance + 1e-06)).reshape(values.shape)

def conv_grid(image, weight):
    return lax.conv_general_dilated(image.astype(jnp.float32), weight.astype(jnp.float32), (1, 1), 'SAME', dimension_numbers=('NHWC', 'HWIO', 'NHWC'), precision=lax.Precision.HIGHEST)

def reference(latents, w_in, w_time, w_first, w_second):
    summed = jnp.zeros((CLIPS, LF, POS, CH), jnp.float32)
    for offset in range(3):
        picked = latents[:, causal_taps(LF, offset)]
        summed = summed + jnp.einsum('clqp,qh->clph', picked.astype(jnp.float32), w_in[offset].astype(jnp.float32), precision=lax.Precision.HIGHEST)
    lat_feats = summed.astype(jnp.bfloat16)
    upsampled = jnp.repeat(lat_feats, UPS, axis=1)
    activated = jax.nn.silu(upsampled.astype(jnp.float32)).astype(jnp.bfloat16)
    mixed = upsampled.astype(jnp.float32)
    for offset in range(3):
        shifted = activated[:, causal_taps(FR, offset)]
        mixed = mixed + jnp.einsum('cfph,hg->cfpg', shifted.astype(jnp.float32), w_time[offset].astype(jnp.float32), precision=lax.Precision.HIGHEST)
    temporal = mixed.astype(jnp.bfloat16).reshape(FRAMES, HS, W, CH)
    first_in = jax.nn.silu(group_norm(temporal.astype(jnp.float32))).astype(jnp.bfloat16)
    inner = conv_grid(first_in, w_first).astype(jnp.bfloat16)
    second_in = jax.nn.silu(group_norm(inner.astype(jnp.float32))).astype(jnp.bfloat16)
    return (temporal.astype(jnp.float32) + conv_grid(second_in, w_second)).astype(jnp.bfloat16)
```

```python
import jax
import jax.numpy as jnp
from jax import lax
from jax.sharding import PartitionSpec as P

CH = 512
LATC = 4
GROUPS = 32
HS = 4
W = 160
CLIPS = 4
LF = 8
UPS = 4


def pick(values, places):
    return jnp.stack(
        [
            lax.dynamic_index_in_dim(values, places[i], 0, keepdims=False)
            for i in range(places.shape[0])
        ]
    )


def latent_features(picked, w_in):
    total = jnp.einsum("nqp,qh->nph", picked[0], w_in[0], preferred_element_type=jnp.float32)
    for offset in range(1, 3):
        total = total + jnp.einsum(
            "nqp,qh->nph", picked[offset], w_in[offset], preferred_element_type=jnp.float32
        )
    return total.astype(jnp.bfloat16)


def time_mix(features, residual_feats, weights, own_index, tap_index):
    activated = jax.nn.silu(features.astype(jnp.float32)).astype(jnp.bfloat16)
    total = pick(residual_feats, own_index).astype(jnp.float32)
    for offset in range(3):
        product = jnp.einsum(
            "nph,hg->npg", activated, weights[offset], preferred_element_type=jnp.float32
        )
        total = total + pick(product, tap_index[offset])
    return total.astype(jnp.bfloat16)


def grid_conv(image, weight, total):
    height = image.shape[1]
    width = image.shape[2]
    padded = jnp.pad(image, ((0, 0), (1, 1), (1, 1), (0, 0)))
    for row_off in range(3):
        for col_off in range(3):
            window = padded[:, row_off : row_off + height, col_off : col_off + width]
            total = total + jnp.einsum(
                "fhwk,ko->fhwo",
                window,
                weight[row_off, col_off],
                preferred_element_type=jnp.float32,
            )
    return total


def normed(values):
    group_width = CH // GROUPS
    frames, cells, channels = values.shape
    grouped = values.reshape(frames, cells, channels // group_width, group_width)
    mean = jnp.mean(grouped, axis=(1, 3), keepdims=True)
    centered = grouped - mean
    variance = jnp.mean(centered * centered, axis=(1, 3), keepdims=True)
    scaled = centered * lax.rsqrt(variance + 1e-06)
    return jax.nn.silu(scaled).reshape(values.shape).astype(jnp.bfloat16)


def per_device_channels(latents, w_in, w_time, w_first, w_second):
    rows_count = lax.axis_size("rows")
    quarter = w_first.shape[3]
    channels = w_time.shape[2]
    section_at = lax.axis_index("section")
    clip_frames = LF * UPS
    frames_dev = CLIPS * clip_frames // rows_count
    total_cells = HS * W
    empty_sum = jnp.zeros((frames_dev, HS, W, quarter), jnp.float32)
    gathered = lax.all_gather(latents, "rows", axis=3, tiled=True)
    flat_latents = gathered.reshape(CLIPS * LF, LATC, total_cells)
    first_frame = lax.axis_index("rows") * frames_dev
    clip_at = first_frame // clip_frames
    start_frame = first_frame % clip_frames
    window_len = min(LF, (frames_dev + 1) // UPS + 2)
    window_low = jnp.minimum(jnp.maximum(start_frame - 2, 0) // UPS, LF - window_len)
    window_ids = window_low + jnp.arange(window_len, dtype=jnp.int32)
    picked = [
        pick(flat_latents, clip_at * LF + jnp.maximum(window_ids - 2 + offset, 0))
        for offset in range(3)
    ]
    features = latent_features(picked, w_in)
    frame_ids = start_frame + jnp.arange(frames_dev, dtype=jnp.int32)
    own_index = frame_ids // UPS - window_low
    tap_index = [jnp.maximum(frame_ids - 2 + offset, 0) // UPS - window_low for offset in range(3)]
    framed = time_mix(features, features, w_time, own_index, tap_index)
    first_in = normed(framed.astype(jnp.float32)).reshape(frames_dev, HS, W, channels)
    residual = lax.dynamic_slice_in_dim(framed, section_at * quarter, quarter, 2)
    inner = grid_conv(first_in, w_first, empty_sum)
    inner_cast = inner.astype(jnp.bfloat16).reshape(frames_dev, total_cells, quarter)
    second_in = normed(inner_cast.astype(jnp.float32)).reshape(frames_dev, HS, W, quarter)
    folded = grid_conv(
        lax.all_gather(second_in, "section", axis=3, tiled=True), w_second, empty_sum
    )
    output = residual.reshape(frames_dev, HS, W, quarter).astype(jnp.float32) + folded
    return output.astype(jnp.bfloat16)


def channel_norm(values):
    frames, height, width, channels = values.shape
    group_width = CH // GROUPS
    count = height * width * group_width

    def group_mean(cellwise):
        per_channel = jnp.sum(cellwise, axis=(1, 2))
        per_group = jnp.sum(per_channel.reshape(frames, channels // group_width, group_width), axis=2)
        return jnp.repeat(per_group / count, group_width, axis=1).reshape(frames, 1, 1, channels)

    centered = values - group_mean(values)
    variance = group_mean(centered * centered)
    return jax.nn.silu(centered * lax.rsqrt(variance + 1e-06)).astype(jnp.bfloat16)


def spatial_conv(image, weight):
    return lax.conv_general_dilated(
        image,
        weight,
        (1, 1),
        "SAME",
        dimension_numbers=("NHWC", "HWIO", "NHWC"),
        preferred_element_type=jnp.float32,
    )


def whole_weight(weight):
    rows_count = lax.axis_size("rows")
    core = lax.axis_index("rows") % 2
    half = weight.shape[2] // 2
    mine = lax.dynamic_slice_in_dim(weight, core * half, half, 2)
    mine = lax.all_gather(mine, "section", axis=0, tiled=False)
    other = lax.ppermute(mine, "rows", [(i, i ^ 1) for i in range(rows_count)])
    low = jnp.where(core == 0, mine, other)
    high = jnp.where(core == 0, other, mine)
    full = jnp.concatenate([low, high], axis=3)
    return jnp.moveaxis(full, 0, 3).reshape(weight.shape[:3] + (-1,))


def unique_frames(latents, w_in, w_time, own):
    gathered = lax.all_gather(latents, "rows", axis=3, tiled=True)
    flat_latents = gathered.reshape(CLIPS * LF, LATC, HS * W)
    clip = own // LF
    at = own % LF
    count = own.shape[0]
    places = jnp.concatenate([jnp.maximum(at - 1, 0), at])
    taps = jnp.maximum(places[:, None] - 2 + jnp.arange(3, dtype=jnp.int32), 0)
    taps = taps + jnp.concatenate([clip, clip])[:, None] * LF
    picked = pick(flat_latents, taps.reshape(-1))
    picked = picked.reshape(2 * count, 3 * LATC, HS * W)
    features = jnp.einsum(
        "nqp,qh->nph", picked, w_in.reshape(3 * LATC, -1), preferred_element_type=jnp.float32
    ).astype(jnp.bfloat16)
    activated = jax.nn.silu(features.astype(jnp.float32)).astype(jnp.bfloat16)
    before, now = activated[:count], activated[count:]
    stacked = jnp.stack(
        [
            jnp.concatenate([before, before, now], axis=2),
            jnp.concatenate([before, now, now], axis=2),
            jnp.concatenate([now, now, now], axis=2),
        ]
    )
    mixed = jnp.einsum(
        "jnpk,kg->jnpg",
        stacked,
        w_time.reshape(-1, w_time.shape[2]),
        preferred_element_type=jnp.float32,
    )
    mixed = mixed + features[count:].astype(jnp.float32)
    return mixed.astype(jnp.bfloat16).reshape(3, count, HS, W, -1)


def per_device_frames(latents, w_in, w_time, w_first, w_second):
    sections = lax.axis_size("section")
    rows_count = lax.axis_size("rows")
    section_at = lax.axis_index("section")
    quarter = w_first.shape[3]
    count = CLIPS * LF // rows_count // sections
    first = (lax.axis_index("rows") * sections + section_at) * count
    own = first + jnp.arange(count, dtype=jnp.int32)
    full_first = whole_weight(w_first)
    full_second = whole_weight(w_second)
    framed = unique_frames(latents, w_in, w_time, own)
    flat = framed.reshape((3 * count,) + framed.shape[2:])
    inner = spatial_conv(channel_norm(flat.astype(jnp.float32)), full_first).astype(jnp.bfloat16)
    second_in = channel_norm(inner.astype(jnp.float32)).reshape(framed.shape)
    arrived = []
    for frame in range(3):
        out = framed[frame].astype(jnp.float32) + spatial_conv(second_in[frame], full_second)
        out = out.astype(jnp.bfloat16)
        parts = []
        for hop in range(sections):
            part = lax.dynamic_slice_in_dim(out, (section_at ^ hop) * quarter, quarter, 3)
            if hop > 0:
                part = lax.ppermute(part, "section", [(i, i ^ hop) for i in range(sections)])
            parts.append(part)
        arrived.append(parts)
    placed = []
    for sender in range(sections):
        frames = [
            lax.select_n(section_at, *[arrived[f][sender ^ s] for s in range(sections)])
            for f in range(3)
        ]
        placed.append(jnp.stack(frames + [frames[2]], axis=1))
    result = jnp.concatenate(placed, axis=0)
    return result.reshape((sections * count * UPS, HS, W, quarter))


def per_device(latents, w_in, w_time, w_first, w_second):
    sections = lax.axis_size("section")
    rows_count = lax.axis_size("rows")
    even = (CLIPS * LF) % (rows_count * sections) == 0
    if even and rows_count % 2 == 0 and sections & (sections - 1) == 0:
        return per_device_frames(latents, w_in, w_time, w_first, w_second)
    return per_device_channels(latents, w_in, w_time, w_first, w_second)


def solution(mesh):
    in_specs = (
        P(None, None, None, "rows"),
        P(),
        P(),
        P(None, None, None, "section"),
        P(None, None, None, "section"),
    )
    out_specs = P("rows", None, None, "section")
    return jax.shard_map(
        per_device, mesh=mesh, in_specs=in_specs, out_specs=out_specs, check_vma=False
    )
```

```python
import functools

import jax
import jax.numpy as jnp
from jax import lax
from jax.experimental import pallas as pl
from jax.experimental.pallas import tpu as pltpu
from jax.sharding import PartitionSpec as P

CH = 512
LATC = 4
GROUPS = 32
HS = 4
W = 160
CLIPS = 4
LF = 8
UPS = 4


def pick(values, places):
    return jnp.stack(
        [
            lax.dynamic_index_in_dim(values, places[i], 0, keepdims=False)
            for i in range(places.shape[0])
        ]
    )


def latent_features(picked, w_in):
    total = jnp.einsum("nqp,qh->nph", picked[0], w_in[0], preferred_element_type=jnp.float32)
    for offset in range(1, 3):
        total = total + jnp.einsum(
            "nqp,qh->nph", picked[offset], w_in[offset], preferred_element_type=jnp.float32
        )
    return total.astype(jnp.bfloat16)


def time_mix(features, residual_feats, weights, own_index, tap_index):
    activated = jax.nn.silu(features.astype(jnp.float32)).astype(jnp.bfloat16)
    total = pick(residual_feats, own_index).astype(jnp.float32)
    for offset in range(3):
        product = jnp.einsum(
            "nph,hg->npg", activated, weights[offset], preferred_element_type=jnp.float32
        )
        total = total + pick(product, tap_index[offset])
    return total.astype(jnp.bfloat16)


def grid_conv(image, weight, total):
    height = image.shape[1]
    width = image.shape[2]
    padded = jnp.pad(image, ((0, 0), (1, 1), (1, 1), (0, 0)))
    for row_off in range(3):
        for col_off in range(3):
            window = padded[:, row_off : row_off + height, col_off : col_off + width]
            total = total + jnp.einsum(
                "fhwk,ko->fhwo",
                window,
                weight[row_off, col_off],
                preferred_element_type=jnp.float32,
            )
    return total


def normed(values):
    group_width = CH // GROUPS
    frames, cells, channels = values.shape
    grouped = values.reshape(frames, cells, channels // group_width, group_width)
    mean = jnp.mean(grouped, axis=(1, 3), keepdims=True)
    centered = grouped - mean
    variance = jnp.mean(centered * centered, axis=(1, 3), keepdims=True)
    scaled = centered * lax.rsqrt(variance + 1e-06)
    return jax.nn.silu(scaled).reshape(values.shape).astype(jnp.bfloat16)


def per_device_channels(latents, w_in, w_time, w_first, w_second):
    rows_count = lax.axis_size("rows")
    quarter = w_first.shape[3]
    channels = w_time.shape[2]
    section_at = lax.axis_index("section")
    clip_frames = LF * UPS
    frames_dev = CLIPS * clip_frames // rows_count
    total_cells = HS * W
    empty_sum = jnp.zeros((frames_dev, HS, W, quarter), jnp.float32)
    gathered = lax.all_gather(latents, "rows", axis=3, tiled=True)
    flat_latents = gathered.reshape(CLIPS * LF, LATC, total_cells)
    first_frame = lax.axis_index("rows") * frames_dev
    clip_at = first_frame // clip_frames
    start_frame = first_frame % clip_frames
    window_len = min(LF, (frames_dev + 1) // UPS + 2)
    window_low = jnp.minimum(jnp.maximum(start_frame - 2, 0) // UPS, LF - window_len)
    window_ids = window_low + jnp.arange(window_len, dtype=jnp.int32)
    picked = [
        pick(flat_latents, clip_at * LF + jnp.maximum(window_ids - 2 + offset, 0))
        for offset in range(3)
    ]
    features = latent_features(picked, w_in)
    frame_ids = start_frame + jnp.arange(frames_dev, dtype=jnp.int32)
    own_index = frame_ids // UPS - window_low
    tap_index = [jnp.maximum(frame_ids - 2 + offset, 0) // UPS - window_low for offset in range(3)]
    framed = time_mix(features, features, w_time, own_index, tap_index)
    first_in = normed(framed.astype(jnp.float32)).reshape(frames_dev, HS, W, channels)
    residual = lax.dynamic_slice_in_dim(framed, section_at * quarter, quarter, 2)
    inner = grid_conv(first_in, w_first, empty_sum)
    inner_cast = inner.astype(jnp.bfloat16).reshape(frames_dev, total_cells, quarter)
    second_in = normed(inner_cast.astype(jnp.float32)).reshape(frames_dev, HS, W, quarter)
    folded = grid_conv(
        lax.all_gather(second_in, "section", axis=3, tiled=True), w_second, empty_sum
    )
    output = residual.reshape(frames_dev, HS, W, quarter).astype(jnp.float32) + folded
    return output.astype(jnp.bfloat16)


def norm_conv_kernel(split, core_ref, image_ref, mine_ref, other_ref, *rest):
    residual_ref = rest[0] if len(rest) == 4 else None
    out_ref, full_ref, padded_ref = rest[-3:]
    sections, taps, half, quarter = mine_ref.shape
    cells, channels = image_ref.shape[1:]
    group_width = CH // GROUPS

    @pl.when(pl.program_id(0) == 0)
    def _():
        core = core_ref[0]

        @pl.loop(0, taps)
        def _(tap):
            for ref, at in ((mine_ref, core), (other_ref, 1 - core)):
                rows = pl.ds(pl.multiple_of(tap * channels + at * half, half), half)
                for section in range(sections):
                    lanes = slice(section * quarter, (section + 1) * quarter)
                    full_ref[rows, lanes] = ref[section, tap]

        edge = jnp.zeros((W, 3 * channels), jnp.bfloat16)
        padded_ref[:W, :] = edge
        padded_ref[W + cells :, :] = edge

    row_group = lax.div(lax.broadcasted_iota(jnp.int32, (channels, channels), 0), group_width)
    col_group = lax.div(lax.broadcasted_iota(jnp.int32, (channels, channels), 1), group_width)
    same = jnp.where(row_group == col_group, 1.0, 0.0).astype(jnp.float32)

    def group_mean(cellwise):
        per_channel = jnp.sum(cellwise, axis=0, keepdims=True)
        total = jnp.dot(
            jnp.broadcast_to(per_channel, (8, channels)),
            same,
            precision=lax.Precision.HIGHEST,
            preferred_element_type=jnp.float32,
        )
        return total[:1] * (1.0 / (cells * group_width))

    values = image_ref[0].astype(jnp.float32)
    centered = values - group_mean(values)
    scaled = centered * lax.rsqrt(group_mean(centered * centered) + 1e-06)
    active = scaled / (1.0 + jnp.exp(-scaled))
    column = lax.rem(lax.broadcasted_iota(jnp.int32, (cells, channels), 0), W)
    inside = slice(W, W + cells)
    left = jnp.where(column == 0, 0.0, pltpu.roll(active, 1, 0))
    right = jnp.where(column == W - 1, 0.0, pltpu.roll(active, cells - 1, 0))
    padded_ref[inside, :channels] = left.astype(jnp.bfloat16)
    padded_ref[inside, channels : 2 * channels] = active.astype(jnp.bfloat16)
    padded_ref[inside, 2 * channels :] = right.astype(jnp.bfloat16)

    depth = 3 * channels
    width = 2 * quarter
    for block in range(channels // width):
        lanes = slice(block * width, (block + 1) * width)
        total = None
        for row_off in range(3):
            product = jnp.dot(
                padded_ref[row_off * W : row_off * W + cells, :],
                full_ref[row_off * depth : (row_off + 1) * depth, lanes],
                preferred_element_type=jnp.float32,
            )
            total = product if total is None else total + product
        if residual_ref is not None:
            total = total + residual_ref[0, :, lanes].astype(jnp.float32)
        total = total.astype(jnp.bfloat16)
        if split:
            out_ref[0, 2 * block] = total[:, :quarter]
            out_ref[0, 2 * block + 1] = total[:, quarter:]
        else:
            out_ref[0, :, lanes] = total


def norm_conv(image, halves, core, residual=None):
    frames, cells, channels = image.shape
    mine, other = halves
    sections, taps, half, quarter = mine.shape
    split = residual is not None
    frame_spec = pl.BlockSpec((1, cells, channels), lambda i: (i, 0, 0))
    weight_spec = pl.BlockSpec(mine.shape, lambda i: (0, 0, 0, 0))
    in_specs = [pl.BlockSpec(memory_space=pltpu.SMEM), frame_spec, weight_spec, weight_spec]
    operands = [core.reshape(1), image, mine, other]
    out_shape, out_spec = (frames, cells, channels), frame_spec
    if split:
        in_specs.append(frame_spec)
        operands.append(residual)
        out_shape = (frames, sections, cells, quarter)
        out_spec = pl.BlockSpec((1, sections, cells, quarter), lambda i: (i, 0, 0, 0))
    return pl.pallas_call(
        functools.partial(norm_conv_kernel, split),
        grid=(frames,),
        in_specs=in_specs,
        out_specs=out_spec,
        out_shape=jax.ShapeDtypeStruct(out_shape, jnp.bfloat16),
        scratch_shapes=[
            pltpu.VMEM((taps * channels, sections * quarter), jnp.bfloat16),
            pltpu.VMEM((cells + 2 * W, 3 * channels), jnp.bfloat16),
        ],
        compiler_params=pltpu.CompilerParams(vmem_limit_bytes=50 * 1024 * 1024),
        cost_estimate=pl.CostEstimate(
            flops=2 * frames * cells * taps * channels * channels,
            bytes_accessed=2 * taps * channels * channels + 4 * frames * cells * channels,
            transcendentals=frames * cells * channels,
        ),
    )(*operands)


def weight_halves(weight, core):
    rows_count = lax.axis_size("rows")
    half = weight.shape[2] // 2
    mine = lax.dynamic_slice_in_dim(weight, core * half, half, 2)
    mine = mine.reshape((9,) + mine.shape[2:])
    mine = lax.all_gather(mine, "section", axis=0, tiled=False)
    other = lax.ppermute(mine, "rows", [(i, i ^ 1) for i in range(rows_count)])
    return mine, other


def unique_frames(latents, w_in, w_time, own):
    gathered = lax.all_gather(latents, "rows", axis=3, tiled=True)
    flat_latents = gathered.reshape(CLIPS * LF, LATC, HS * W)
    clip = own // LF
    at = own % LF
    count = own.shape[0]
    places = jnp.concatenate([jnp.maximum(at - 1, 0), at])
    taps = jnp.maximum(places[:, None] - 2 + jnp.arange(3, dtype=jnp.int32), 0)
    taps = taps + jnp.concatenate([clip, clip])[:, None] * LF
    picked = pick(flat_latents, taps.reshape(-1))
    picked = picked.reshape(2 * count, 3 * LATC, HS * W)
    features = jnp.einsum(
        "nqp,qh->nph", picked, w_in.reshape(3 * LATC, -1), preferred_element_type=jnp.float32
    ).astype(jnp.bfloat16)
    activated = jax.nn.silu(features.astype(jnp.float32)).astype(jnp.bfloat16)
    before, now = activated[:count], activated[count:]
    stacked = jnp.stack(
        [
            jnp.concatenate([before, before, now], axis=2),
            jnp.concatenate([before, now, now], axis=2),
            jnp.concatenate([now, now, now], axis=2),
        ]
    )
    mixed = jnp.einsum(
        "jnpk,kg->jnpg",
        stacked,
        w_time.reshape(-1, w_time.shape[2]),
        preferred_element_type=jnp.float32,
    )
    mixed = mixed + features[count:].astype(jnp.float32)
    return mixed.astype(jnp.bfloat16)


def per_device_frames(latents, w_in, w_time, w_first, w_second):
    sections = lax.axis_size("section")
    rows_count = lax.axis_size("rows")
    section_at = lax.axis_index("section")
    quarter = w_first.shape[3]
    count = CLIPS * LF // rows_count // sections
    first = (lax.axis_index("rows") * sections + section_at) * count
    own = first + jnp.arange(count, dtype=jnp.int32)
    core = lax.axis_index("rows") % 2
    first_halves = weight_halves(w_first, core)
    second_halves = weight_halves(w_second, core)
    framed = unique_frames(latents, w_in, w_time, own)
    cells, channels = framed.shape[2:]
    inner = norm_conv(framed.reshape(3 * count, cells, channels), first_halves, core)
    inner = inner.reshape(framed.shape)
    arrived = []
    for frame in range(3):
        out = norm_conv(inner[frame], second_halves, core, framed[frame])
        parts = []
        for hop in range(sections):
            part = lax.dynamic_index_in_dim(out, section_at ^ hop, 1, keepdims=False)
            if hop > 0:
                part = lax.ppermute(part, "section", [(i, i ^ hop) for i in range(sections)])
            parts.append(part)
        arrived.append(parts)
    placed = []
    for sender in range(sections):
        frames = [
            lax.select_n(section_at, *[arrived[f][sender ^ s] for s in range(sections)])
            for f in range(3)
        ]
        placed.append(jnp.stack(frames + [frames[2]], axis=1))
    result = jnp.concatenate(placed, axis=0)
    return result.reshape((sections * count * UPS, HS, W, quarter))


def per_device(latents, w_in, w_time, w_first, w_second):
    sections = lax.axis_size("section")
    rows_count = lax.axis_size("rows")
    even = (CLIPS * LF) % (rows_count * sections) == 0
    if even and rows_count % 2 == 0 and sections > 1 and sections & (sections - 1) == 0:
        return per_device_frames(latents, w_in, w_time, w_first, w_second)
    return per_device_channels(latents, w_in, w_time, w_first, w_second)


def solution(mesh):
    in_specs = (
        P(None, None, None, "rows"),
        P(),
        P(),
        P(None, None, None, "section"),
        P(None, None, None, "section"),
    )
    out_specs = P("rows", None, None, "section")
    return jax.shard_map(
        per_device, mesh=mesh, in_specs=in_specs, out_specs=out_specs, check_vma=False
    )
```

```python
import functools

import jax
import jax.numpy as jnp
from jax import lax
from jax.experimental import pallas as pl
from jax.experimental.pallas import tpu as pltpu
from jax.sharding import PartitionSpec as P

CH = 512
LATC = 4
GROUPS = 32
HS = 4
W = 160
CLIPS = 4
LF = 8
UPS = 4


def pick(values, places):
    return jnp.stack(
        [
            lax.dynamic_index_in_dim(values, places[i], 0, keepdims=False)
            for i in range(places.shape[0])
        ]
    )


def latent_features(picked, w_in):
    total = jnp.einsum("nqp,qh->nph", picked[0], w_in[0], preferred_element_type=jnp.float32)
    for offset in range(1, 3):
        total = total + jnp.einsum(
            "nqp,qh->nph", picked[offset], w_in[offset], preferred_element_type=jnp.float32
        )
    return total.astype(jnp.bfloat16)


def time_mix(features, residual_feats, weights, own_index, tap_index):
    activated = jax.nn.silu(features.astype(jnp.float32)).astype(jnp.bfloat16)
    total = pick(residual_feats, own_index).astype(jnp.float32)
    for offset in range(3):
        product = jnp.einsum(
            "nph,hg->npg", activated, weights[offset], preferred_element_type=jnp.float32
        )
        total = total + pick(product, tap_index[offset])
    return total.astype(jnp.bfloat16)


def grid_conv(image, weight, total):
    height = image.shape[1]
    width = image.shape[2]
    padded = jnp.pad(image, ((0, 0), (1, 1), (1, 1), (0, 0)))
    for row_off in range(3):
        for col_off in range(3):
            window = padded[:, row_off : row_off + height, col_off : col_off + width]
            total = total + jnp.einsum(
                "fhwk,ko->fhwo",
                window,
                weight[row_off, col_off],
                preferred_element_type=jnp.float32,
            )
    return total


def normed(values):
    group_width = CH // GROUPS
    frames, cells, channels = values.shape
    grouped = values.reshape(frames, cells, channels // group_width, group_width)
    mean = jnp.mean(grouped, axis=(1, 3), keepdims=True)
    centered = grouped - mean
    variance = jnp.mean(centered * centered, axis=(1, 3), keepdims=True)
    scaled = centered * lax.rsqrt(variance + 1e-06)
    return jax.nn.silu(scaled).reshape(values.shape).astype(jnp.bfloat16)


def per_device_channels(latents, w_in, w_time, w_first, w_second):
    rows_count = lax.axis_size("rows")
    quarter = w_first.shape[3]
    channels = w_time.shape[2]
    section_at = lax.axis_index("section")
    clip_frames = LF * UPS
    frames_dev = CLIPS * clip_frames // rows_count
    total_cells = HS * W
    empty_sum = jnp.zeros((frames_dev, HS, W, quarter), jnp.float32)
    gathered = lax.all_gather(latents, "rows", axis=3, tiled=True)
    flat_latents = gathered.reshape(CLIPS * LF, LATC, total_cells)
    first_frame = lax.axis_index("rows") * frames_dev
    clip_at = first_frame // clip_frames
    start_frame = first_frame % clip_frames
    window_len = min(LF, (frames_dev + 1) // UPS + 2)
    window_low = jnp.minimum(jnp.maximum(start_frame - 2, 0) // UPS, LF - window_len)
    window_ids = window_low + jnp.arange(window_len, dtype=jnp.int32)
    picked = [
        pick(flat_latents, clip_at * LF + jnp.maximum(window_ids - 2 + offset, 0))
        for offset in range(3)
    ]
    features = latent_features(picked, w_in)
    frame_ids = start_frame + jnp.arange(frames_dev, dtype=jnp.int32)
    own_index = frame_ids // UPS - window_low
    tap_index = [jnp.maximum(frame_ids - 2 + offset, 0) // UPS - window_low for offset in range(3)]
    framed = time_mix(features, features, w_time, own_index, tap_index)
    first_in = normed(framed.astype(jnp.float32)).reshape(frames_dev, HS, W, channels)
    residual = lax.dynamic_slice_in_dim(framed, section_at * quarter, quarter, 2)
    inner = grid_conv(first_in, w_first, empty_sum)
    inner_cast = inner.astype(jnp.bfloat16).reshape(frames_dev, total_cells, quarter)
    second_in = normed(inner_cast.astype(jnp.float32)).reshape(frames_dev, HS, W, quarter)
    folded = grid_conv(
        lax.all_gather(second_in, "section", axis=3, tiled=True), w_second, empty_sum
    )
    output = residual.reshape(frames_dev, HS, W, quarter).astype(jnp.float32) + folded
    return output.astype(jnp.bfloat16)


def norm_conv_kernel(split, core_ref, image_ref, mine_ref, other_ref, *rest):
    residual_ref = rest[0] if len(rest) == 4 else None
    out_ref, full_ref, padded_ref = rest[-3:]
    sections, taps, half, quarter = mine_ref.shape
    cells, channels = image_ref.shape[1:]
    group_width = CH // GROUPS

    @pl.when(pl.program_id(0) == 0)
    def _():
        core = core_ref[0]

        @pl.loop(0, taps)
        def _(tap):
            for ref, at in ((mine_ref, core), (other_ref, 1 - core)):
                rows = pl.ds(pl.multiple_of(tap * channels + at * half, half), half)
                for section in range(sections):
                    lanes = slice(section * quarter, (section + 1) * quarter)
                    full_ref[rows, lanes] = ref[section, tap]

        edge = jnp.zeros((W, 3 * channels), jnp.bfloat16)
        padded_ref[:W, :] = edge
        padded_ref[W + cells :, :] = edge

    row_group = lax.div(lax.broadcasted_iota(jnp.int32, (channels, channels), 0), group_width)
    col_group = lax.div(lax.broadcasted_iota(jnp.int32, (channels, channels), 1), group_width)
    same = jnp.where(row_group == col_group, 1.0, 0.0).astype(jnp.float32)

    def group_mean(cellwise):
        per_channel = jnp.sum(cellwise, axis=0, keepdims=True)
        total = jnp.dot(
            jnp.broadcast_to(per_channel, (8, channels)),
            same,
            precision=lax.Precision.HIGHEST,
            preferred_element_type=jnp.float32,
        )
        return total[:1] * (1.0 / (cells * group_width))

    values = image_ref[0].astype(jnp.float32)
    centered = values - group_mean(values)
    scaled = centered * lax.rsqrt(group_mean(centered * centered) + 1e-06)
    active = scaled / (1.0 + jnp.exp(-scaled))
    column = lax.rem(lax.broadcasted_iota(jnp.int32, (cells, channels), 0), W)
    inside = slice(W, W + cells)
    left = jnp.where(column == 0, 0.0, pltpu.roll(active, 1, 0))
    right = jnp.where(column == W - 1, 0.0, pltpu.roll(active, cells - 1, 0))
    padded_ref[inside, :channels] = left.astype(jnp.bfloat16)
    padded_ref[inside, channels : 2 * channels] = active.astype(jnp.bfloat16)
    padded_ref[inside, 2 * channels :] = right.astype(jnp.bfloat16)

    depth = 3 * channels
    width = 2 * quarter
    for block in range(channels // width):
        lanes = slice(block * width, (block + 1) * width)
        total = None
        for row_off in range(3):
            product = jnp.dot(
                padded_ref[row_off * W : row_off * W + cells, :],
                full_ref[row_off * depth : (row_off + 1) * depth, lanes],
                preferred_element_type=jnp.float32,
            )
            total = product if total is None else total + product
        if residual_ref is not None:
            total = total + residual_ref[0, :, lanes].astype(jnp.float32)
        total = total.astype(jnp.bfloat16)
        if split:
            out_ref[0, 2 * block] = total[:, :quarter]
            out_ref[0, 2 * block + 1] = total[:, quarter:]
        else:
            out_ref[0, :, lanes] = total


def norm_conv(image, halves, core, residual=None):
    frames, cells, channels = image.shape
    mine, other = halves
    sections, taps, half, quarter = mine.shape
    split = residual is not None
    frame_spec = pl.BlockSpec((1, cells, channels), lambda i: (i, 0, 0))
    weight_spec = pl.BlockSpec(mine.shape, lambda i: (0, 0, 0, 0))
    in_specs = [pl.BlockSpec(memory_space=pltpu.SMEM), frame_spec, weight_spec, weight_spec]
    operands = [core.reshape(1), image, mine, other]
    out_shape, out_spec = (frames, cells, channels), frame_spec
    if split:
        in_specs.append(frame_spec)
        operands.append(residual)
        out_shape = (frames, sections, cells, quarter)
        out_spec = pl.BlockSpec((1, sections, cells, quarter), lambda i: (i, 0, 0, 0))
    return pl.pallas_call(
        functools.partial(norm_conv_kernel, split),
        grid=(frames,),
        in_specs=in_specs,
        out_specs=out_spec,
        out_shape=jax.ShapeDtypeStruct(out_shape, jnp.bfloat16),
        scratch_shapes=[
            pltpu.VMEM((taps * channels, sections * quarter), jnp.bfloat16),
            pltpu.VMEM((cells + 2 * W, 3 * channels), jnp.bfloat16),
        ],
        compiler_params=pltpu.CompilerParams(vmem_limit_bytes=50 * 1024 * 1024),
        cost_estimate=pl.CostEstimate(
            flops=2 * frames * cells * taps * channels * channels,
            bytes_accessed=2 * taps * channels * channels + 4 * frames * cells * channels,
            transcendentals=frames * cells * channels,
        ),
    )(*operands)


def gather_half(weight, core):
    half = weight.shape[2] // 2
    mine = lax.dynamic_slice_in_dim(weight, core * half, half, 2)
    return lax.all_gather(mine.reshape((9,) + mine.shape[2:]), "section", axis=0, tiled=False)


def swap_half(mine):
    rows_count = lax.axis_size("rows")
    return mine, lax.ppermute(mine, "rows", [(i, i ^ 1) for i in range(rows_count)])


def unique_frames(latents, w_in, w_time, own):
    gathered = lax.all_gather(latents, "rows", axis=3, tiled=True)
    flat_latents = gathered.reshape(CLIPS * LF, LATC, HS * W)
    clip = own // LF
    at = own % LF
    count = own.shape[0]
    places = jnp.concatenate([jnp.maximum(at - 1, 0), at])
    taps = jnp.maximum(places[:, None] - 2 + jnp.arange(3, dtype=jnp.int32), 0)
    taps = taps + jnp.concatenate([clip, clip])[:, None] * LF
    picked = pick(flat_latents, taps.reshape(-1))
    picked = picked.reshape(2 * count, 3 * LATC, HS * W)
    features = jnp.einsum(
        "nqp,qh->nph", picked, w_in.reshape(3 * LATC, -1), preferred_element_type=jnp.float32
    ).astype(jnp.bfloat16)
    activated = jax.nn.silu(features.astype(jnp.float32)).astype(jnp.bfloat16)
    before, now = activated[:count], activated[count:]
    stacked = jnp.stack(
        [
            jnp.concatenate([before, before, now], axis=2),
            jnp.concatenate([before, now, now], axis=2),
            jnp.concatenate([now, now, now], axis=2),
        ]
    )
    mixed = jnp.einsum(
        "jnpk,kg->jnpg",
        stacked,
        w_time.reshape(-1, w_time.shape[2]),
        preferred_element_type=jnp.float32,
    )
    mixed = mixed + features[count:].astype(jnp.float32)
    return mixed.astype(jnp.bfloat16)


def per_device_frames(latents, w_in, w_time, w_first, w_second):
    sections = lax.axis_size("section")
    rows_count = lax.axis_size("rows")
    section_at = lax.axis_index("section")
    quarter = w_first.shape[3]
    count = CLIPS * LF // rows_count // sections
    first = (lax.axis_index("rows") * sections + section_at) * count
    own = first + jnp.arange(count, dtype=jnp.int32)
    core = lax.axis_index("rows") % 2
    first_halves = swap_half(gather_half(w_first, core))
    second_mine = gather_half(w_second, core)
    framed = unique_frames(latents, w_in, w_time, own)
    cells, channels = framed.shape[2:]
    early = norm_conv(framed[:2].reshape(2 * count, cells, channels), first_halves, core)
    reached = early[0, 0, 0].astype(jnp.float32) < 1e30
    second_halves = swap_half(jnp.where(reached, second_mine, jnp.zeros_like(second_mine)))
    early = early.reshape(framed[:2].shape)
    inner = [early[0], early[1], norm_conv(framed[2], first_halves, core)]
    arrived = []
    for frame in range(3):
        out = norm_conv(inner[frame], second_halves, core, framed[frame])
        parts = []
        for hop in range(sections):
            part = lax.dynamic_index_in_dim(out, section_at ^ hop, 1, keepdims=False)
            if hop > 0:
                part = lax.ppermute(part, "section", [(i, i ^ hop) for i in range(sections)])
            parts.append(part)
        arrived.append(parts)
    placed = []
    for sender in range(sections):
        frames = [
            lax.select_n(section_at, *[arrived[f][sender ^ s] for s in range(sections)])
            for f in range(3)
        ]
        placed.append(jnp.stack(frames + [frames[2]], axis=1))
    result = jnp.concatenate(placed, axis=0)
    return result.reshape((sections * count * UPS, HS, W, quarter))


def per_device(latents, w_in, w_time, w_first, w_second):
    sections = lax.axis_size("section")
    rows_count = lax.axis_size("rows")
    even = (CLIPS * LF) % (rows_count * sections) == 0
    if even and rows_count % 2 == 0 and sections > 1 and sections & (sections - 1) == 0:
        return per_device_frames(latents, w_in, w_time, w_first, w_second)
    return per_device_channels(latents, w_in, w_time, w_first, w_second)


def solution(mesh):
    in_specs = (
        P(None, None, None, "rows"),
        P(),
        P(),
        P(None, None, None, "section"),
        P(None, None, None, "section"),
    )
    out_specs = P("rows", None, None, "section")
    return jax.shard_map(
        per_device, mesh=mesh, in_specs=in_specs, out_specs=out_specs, check_vma=False
    )
```

```python
import functools

import jax
import jax.numpy as jnp
from jax import lax
from jax.experimental import pallas as pl
from jax.experimental.pallas import tpu as pltpu
from jax.sharding import PartitionSpec as P

CH = 512
LATC = 4
GROUPS = 32
HS = 4
W = 160
CLIPS = 4
LF = 8
UPS = 4


def pick(values, places):
    return jnp.stack(
        [
            lax.dynamic_index_in_dim(values, places[i], 0, keepdims=False)
            for i in range(places.shape[0])
        ]
    )


def latent_features(picked, w_in):
    total = jnp.einsum("nqp,qh->nph", picked[0], w_in[0], preferred_element_type=jnp.float32)
    for offset in range(1, 3):
        total = total + jnp.einsum(
            "nqp,qh->nph", picked[offset], w_in[offset], preferred_element_type=jnp.float32
        )
    return total.astype(jnp.bfloat16)


def time_mix(features, residual_feats, weights, own_index, tap_index):
    activated = jax.nn.silu(features.astype(jnp.float32)).astype(jnp.bfloat16)
    total = pick(residual_feats, own_index).astype(jnp.float32)
    for offset in range(3):
        product = jnp.einsum(
            "nph,hg->npg", activated, weights[offset], preferred_element_type=jnp.float32
        )
        total = total + pick(product, tap_index[offset])
    return total.astype(jnp.bfloat16)


def grid_conv(image, weight, total):
    height = image.shape[1]
    width = image.shape[2]
    padded = jnp.pad(image, ((0, 0), (1, 1), (1, 1), (0, 0)))
    for row_off in range(3):
        for col_off in range(3):
            window = padded[:, row_off : row_off + height, col_off : col_off + width]
            total = total + jnp.einsum(
                "fhwk,ko->fhwo",
                window,
                weight[row_off, col_off],
                preferred_element_type=jnp.float32,
            )
    return total


def normed(values):
    group_width = CH // GROUPS
    frames, cells, channels = values.shape
    grouped = values.reshape(frames, cells, channels // group_width, group_width)
    mean = jnp.mean(grouped, axis=(1, 3), keepdims=True)
    centered = grouped - mean
    variance = jnp.mean(centered * centered, axis=(1, 3), keepdims=True)
    scaled = centered * lax.rsqrt(variance + 1e-06)
    return jax.nn.silu(scaled).reshape(values.shape).astype(jnp.bfloat16)


def per_device_channels(latents, w_in, w_time, w_first, w_second):
    rows_count = lax.axis_size("rows")
    quarter = w_first.shape[3]
    channels = w_time.shape[2]
    section_at = lax.axis_index("section")
    clip_frames = LF * UPS
    frames_dev = CLIPS * clip_frames // rows_count
    total_cells = HS * W
    empty_sum = jnp.zeros((frames_dev, HS, W, quarter), jnp.float32)
    gathered = lax.all_gather(latents, "rows", axis=3, tiled=True)
    flat_latents = gathered.reshape(CLIPS * LF, LATC, total_cells)
    first_frame = lax.axis_index("rows") * frames_dev
    clip_at = first_frame // clip_frames
    start_frame = first_frame % clip_frames
    window_len = min(LF, (frames_dev + 1) // UPS + 2)
    window_low = jnp.minimum(jnp.maximum(start_frame - 2, 0) // UPS, LF - window_len)
    window_ids = window_low + jnp.arange(window_len, dtype=jnp.int32)
    picked = [
        pick(flat_latents, clip_at * LF + jnp.maximum(window_ids - 2 + offset, 0))
        for offset in range(3)
    ]
    features = latent_features(picked, w_in)
    frame_ids = start_frame + jnp.arange(frames_dev, dtype=jnp.int32)
    own_index = frame_ids // UPS - window_low
    tap_index = [jnp.maximum(frame_ids - 2 + offset, 0) // UPS - window_low for offset in range(3)]
    framed = time_mix(features, features, w_time, own_index, tap_index)
    first_in = normed(framed.astype(jnp.float32)).reshape(frames_dev, HS, W, channels)
    residual = lax.dynamic_slice_in_dim(framed, section_at * quarter, quarter, 2)
    inner = grid_conv(first_in, w_first, empty_sum)
    inner_cast = inner.astype(jnp.bfloat16).reshape(frames_dev, total_cells, quarter)
    second_in = normed(inner_cast.astype(jnp.float32)).reshape(frames_dev, HS, W, quarter)
    folded = grid_conv(
        lax.all_gather(second_in, "section", axis=3, tiled=True), w_second, empty_sum
    )
    output = residual.reshape(frames_dev, HS, W, quarter).astype(jnp.float32) + folded
    return output.astype(jnp.bfloat16)


def norm_conv_kernel(split, core_ref, image_ref, mine_ref, other_ref, *rest):
    residual_ref = rest[0] if len(rest) == 4 else None
    out_ref, full_ref, padded_ref = rest[-3:]
    sections, taps, half, quarter = mine_ref.shape
    cells, channels = image_ref.shape[1:]
    group_width = CH // GROUPS

    @pl.when(pl.program_id(0) == 0)
    def _():
        core = core_ref[0]

        @pl.loop(0, taps)
        def _(tap):
            for ref, at in ((mine_ref, core), (other_ref, 1 - core)):
                rows = pl.ds(pl.multiple_of(tap * channels + at * half, half), half)
                for section in range(sections):
                    lanes = slice(section * quarter, (section + 1) * quarter)
                    full_ref[rows, lanes] = ref[section, tap]

        edge = jnp.zeros((W, 3 * channels), jnp.bfloat16)
        padded_ref[:W, :] = edge
        padded_ref[W + cells :, :] = edge

    row_group = lax.div(lax.broadcasted_iota(jnp.int32, (channels, channels), 0), group_width)
    col_group = lax.div(lax.broadcasted_iota(jnp.int32, (channels, channels), 1), group_width)
    same = jnp.where(row_group == col_group, 1.0, 0.0).astype(jnp.float32)

    def group_mean(cellwise):
        per_channel = jnp.sum(cellwise, axis=0, keepdims=True)
        total = jnp.dot(
            jnp.broadcast_to(per_channel, (8, channels)),
            same,
            precision=lax.Precision.HIGHEST,
            preferred_element_type=jnp.float32,
        )
        return total[:1] * (1.0 / (cells * group_width))

    values = image_ref[0].astype(jnp.float32)
    centered = values - group_mean(values)
    scaled = centered * lax.rsqrt(group_mean(centered * centered) + 1e-06)
    active = scaled / (1.0 + jnp.exp(-scaled))
    column = lax.rem(lax.broadcasted_iota(jnp.int32, (cells, channels), 0), W)
    inside = slice(W, W + cells)
    left = jnp.where(column == 0, 0.0, pltpu.roll(active, 1, 0))
    right = jnp.where(column == W - 1, 0.0, pltpu.roll(active, cells - 1, 0))
    padded_ref[inside, :channels] = left.astype(jnp.bfloat16)
    padded_ref[inside, channels : 2 * channels] = active.astype(jnp.bfloat16)
    padded_ref[inside, 2 * channels :] = right.astype(jnp.bfloat16)

    depth = 3 * channels
    width = 2 * quarter
    for block in range(channels // width):
        lanes = slice(block * width, (block + 1) * width)
        total = None
        for row_off in range(3):
            product = jnp.dot(
                padded_ref[row_off * W : row_off * W + cells, :],
                full_ref[row_off * depth : (row_off + 1) * depth, lanes],
                preferred_element_type=jnp.float32,
            )
            total = product if total is None else total + product
        if residual_ref is not None:
            total = total + residual_ref[0, :, lanes].astype(jnp.float32)
        total = total.astype(jnp.bfloat16)
        if split:
            out_ref[0, 2 * block] = total[:, :quarter]
            out_ref[0, 2 * block + 1] = total[:, quarter:]
        else:
            out_ref[0, :, lanes] = total


def norm_conv(image, halves, core, residual=None):
    frames, cells, channels = image.shape
    mine, other = halves
    sections, taps, half, quarter = mine.shape
    split = residual is not None
    frame_spec = pl.BlockSpec((1, cells, channels), lambda i: (i, 0, 0))
    weight_spec = pl.BlockSpec(mine.shape, lambda i: (0, 0, 0, 0))
    in_specs = [pl.BlockSpec(memory_space=pltpu.SMEM), frame_spec, weight_spec, weight_spec]
    operands = [core.reshape(1), image, mine, other]
    out_shape, out_spec = (frames, cells, channels), frame_spec
    if split:
        in_specs.append(frame_spec)
        operands.append(residual)
        out_shape = (frames, sections, cells, quarter)
        out_spec = pl.BlockSpec((1, sections, cells, quarter), lambda i: (i, 0, 0, 0))
    return pl.pallas_call(
        functools.partial(norm_conv_kernel, split),
        grid=(frames,),
        in_specs=in_specs,
        out_specs=out_spec,
        out_shape=jax.ShapeDtypeStruct(out_shape, jnp.bfloat16),
        scratch_shapes=[
            pltpu.VMEM((taps * channels, sections * quarter), jnp.bfloat16),
            pltpu.VMEM((cells + 2 * W, 3 * channels), jnp.bfloat16),
        ],
        compiler_params=pltpu.CompilerParams(vmem_limit_bytes=50 * 1024 * 1024),
        cost_estimate=pl.CostEstimate(
            flops=2 * frames * cells * taps * channels * channels,
            bytes_accessed=2 * taps * channels * channels + 4 * frames * cells * channels,
            transcendentals=frames * cells * channels,
        ),
    )(*operands)


def gather_half(weight, core):
    half = weight.shape[2] // 2
    mine = lax.dynamic_slice_in_dim(weight, core * half, half, 2)
    return lax.all_gather(mine.reshape((9,) + mine.shape[2:]), "section", axis=0, tiled=False)


def permute_half(weight, core):
    sections = lax.axis_size("section")
    section_at = lax.axis_index("section")
    half = weight.shape[2] // 2
    own = lax.dynamic_slice_in_dim(weight, core * half, half, 2)
    own = own.reshape((9,) + own.shape[2:])
    parts = [own] + [
        lax.ppermute(own, "section", [(i, i ^ hop) for i in range(sections)])
        for hop in range(1, sections)
    ]
    return jnp.stack(
        [
            lax.select_n(section_at, *[parts[sender ^ s] for s in range(sections)])
            for sender in range(sections)
        ]
    )


def swap_half(mine):
    rows_count = lax.axis_size("rows")
    return mine, lax.ppermute(mine, "rows", [(i, i ^ 1) for i in range(rows_count)])


def unique_frames(latents, w_in, w_time, own):
    gathered = lax.all_gather(latents, "rows", axis=3, tiled=True)
    flat_latents = gathered.reshape(CLIPS * LF, LATC, HS * W)
    clip = own // LF
    at = own % LF
    count = own.shape[0]
    places = jnp.concatenate([jnp.maximum(at - 1, 0), at])
    taps = jnp.maximum(places[:, None] - 2 + jnp.arange(3, dtype=jnp.int32), 0)
    taps = taps + jnp.concatenate([clip, clip])[:, None] * LF
    picked = pick(flat_latents, taps.reshape(-1))
    picked = picked.reshape(2 * count, 3 * LATC, HS * W)
    features = jnp.einsum(
        "nqp,qh->nph", picked, w_in.reshape(3 * LATC, -1), preferred_element_type=jnp.float32
    ).astype(jnp.bfloat16)
    activated = jax.nn.silu(features.astype(jnp.float32)).astype(jnp.bfloat16)
    before, now = activated[:count], activated[count:]
    stacked = jnp.stack(
        [
            jnp.concatenate([before, before, now], axis=2),
            jnp.concatenate([before, now, now], axis=2),
            jnp.concatenate([now, now, now], axis=2),
        ]
    )
    mixed = jnp.einsum(
        "jnpk,kg->jnpg",
        stacked,
        w_time.reshape(-1, w_time.shape[2]),
        preferred_element_type=jnp.float32,
    )
    mixed = mixed + features[count:].astype(jnp.float32)
    return mixed.astype(jnp.bfloat16)


def per_device_frames(latents, w_in, w_time, w_first, w_second):
    sections = lax.axis_size("section")
    rows_count = lax.axis_size("rows")
    section_at = lax.axis_index("section")
    quarter = w_first.shape[3]
    count = CLIPS * LF // rows_count // sections
    first = (lax.axis_index("rows") * sections + section_at) * count
    own = first + jnp.arange(count, dtype=jnp.int32)
    core = lax.axis_index("rows") % 2
    first_halves = swap_half(gather_half(w_first, core))
    second_halves = swap_half(permute_half(w_second, core))
    framed = unique_frames(latents, w_in, w_time, own)
    cells, channels = framed.shape[2:]
    inner = norm_conv(framed.reshape(3 * count, cells, channels), first_halves, core)
    inner = inner.reshape(framed.shape)
    arrived = []
    for frame in range(3):
        out = norm_conv(inner[frame], second_halves, core, framed[frame])
        parts = []
        for hop in range(sections):
            part = lax.dynamic_index_in_dim(out, section_at ^ hop, 1, keepdims=False)
            if hop > 0:
                part = lax.ppermute(part, "section", [(i, i ^ hop) for i in range(sections)])
            parts.append(part)
        arrived.append(parts)
    placed = []
    for sender in range(sections):
        frames = [
            lax.select_n(section_at, *[arrived[f][sender ^ s] for s in range(sections)])
            for f in range(3)
        ]
        placed.append(jnp.stack(frames + [frames[2]], axis=1))
    result = jnp.concatenate(placed, axis=0)
    return result.reshape((sections * count * UPS, HS, W, quarter))


def per_device(latents, w_in, w_time, w_first, w_second):
    sections = lax.axis_size("section")
    rows_count = lax.axis_size("rows")
    even = (CLIPS * LF) % (rows_count * sections) == 0
    if even and rows_count % 2 == 0 and sections > 1 and sections & (sections - 1) == 0:
        return per_device_frames(latents, w_in, w_time, w_first, w_second)
    return per_device_channels(latents, w_in, w_time, w_first, w_second)


def solution(mesh):
    in_specs = (
        P(None, None, None, "rows"),
        P(),
        P(),
        P(None, None, None, "section"),
        P(None, None, None, "section"),
    )
    out_specs = P("rows", None, None, "section")
    return jax.shard_map(
        per_device, mesh=mesh, in_specs=in_specs, out_specs=out_specs, check_vma=False
    )
```

```python
import functools

import jax
import jax.numpy as jnp
from jax import lax
from jax.experimental import pallas as pl
from jax.experimental.pallas import tpu as pltpu
from jax.sharding import PartitionSpec as P

CH = 512
LATC = 4
GROUPS = 32
HS = 4
W = 160
CLIPS = 4
LF = 8
UPS = 4


def pick(values, places):
    return jnp.stack(
        [
            lax.dynamic_index_in_dim(values, places[i], 0, keepdims=False)
            for i in range(places.shape[0])
        ]
    )


def latent_features(picked, w_in):
    total = jnp.einsum("nqp,qh->nph", picked[0], w_in[0], preferred_element_type=jnp.float32)
    for offset in range(1, 3):
        total = total + jnp.einsum(
            "nqp,qh->nph", picked[offset], w_in[offset], preferred_element_type=jnp.float32
        )
    return total.astype(jnp.bfloat16)


def time_mix(features, residual_feats, weights, own_index, tap_index):
    activated = jax.nn.silu(features.astype(jnp.float32)).astype(jnp.bfloat16)
    total = pick(residual_feats, own_index).astype(jnp.float32)
    for offset in range(3):
        product = jnp.einsum(
            "nph,hg->npg", activated, weights[offset], preferred_element_type=jnp.float32
        )
        total = total + pick(product, tap_index[offset])
    return total.astype(jnp.bfloat16)


def grid_conv(image, weight, total):
    height = image.shape[1]
    width = image.shape[2]
    padded = jnp.pad(image, ((0, 0), (1, 1), (1, 1), (0, 0)))
    for row_off in range(3):
        for col_off in range(3):
            window = padded[:, row_off : row_off + height, col_off : col_off + width]
            total = total + jnp.einsum(
                "fhwk,ko->fhwo",
                window,
                weight[row_off, col_off],
                preferred_element_type=jnp.float32,
            )
    return total


def normed(values):
    group_width = CH // GROUPS
    frames, cells, channels = values.shape
    grouped = values.reshape(frames, cells, channels // group_width, group_width)
    mean = jnp.mean(grouped, axis=(1, 3), keepdims=True)
    centered = grouped - mean
    variance = jnp.mean(centered * centered, axis=(1, 3), keepdims=True)
    scaled = centered * lax.rsqrt(variance + 1e-06)
    return jax.nn.silu(scaled).reshape(values.shape).astype(jnp.bfloat16)


def per_device_channels(latents, w_in, w_time, w_first, w_second):
    rows_count = lax.axis_size("rows")
    quarter = w_first.shape[3]
    channels = w_time.shape[2]
    section_at = lax.axis_index("section")
    clip_frames = LF * UPS
    frames_dev = CLIPS * clip_frames // rows_count
    total_cells = HS * W
    empty_sum = jnp.zeros((frames_dev, HS, W, quarter), jnp.float32)
    gathered = lax.all_gather(latents, "rows", axis=3, tiled=True)
    flat_latents = gathered.reshape(CLIPS * LF, LATC, total_cells)
    first_frame = lax.axis_index("rows") * frames_dev
    clip_at = first_frame // clip_frames
    start_frame = first_frame % clip_frames
    window_len = min(LF, (frames_dev + 1) // UPS + 2)
    window_low = jnp.minimum(jnp.maximum(start_frame - 2, 0) // UPS, LF - window_len)
    window_ids = window_low + jnp.arange(window_len, dtype=jnp.int32)
    picked = [
        pick(flat_latents, clip_at * LF + jnp.maximum(window_ids - 2 + offset, 0))
        for offset in range(3)
    ]
    features = latent_features(picked, w_in)
    frame_ids = start_frame + jnp.arange(frames_dev, dtype=jnp.int32)
    own_index = frame_ids // UPS - window_low
    tap_index = [jnp.maximum(frame_ids - 2 + offset, 0) // UPS - window_low for offset in range(3)]
    framed = time_mix(features, features, w_time, own_index, tap_index)
    first_in = normed(framed.astype(jnp.float32)).reshape(frames_dev, HS, W, channels)
    residual = lax.dynamic_slice_in_dim(framed, section_at * quarter, quarter, 2)
    inner = grid_conv(first_in, w_first, empty_sum)
    inner_cast = inner.astype(jnp.bfloat16).reshape(frames_dev, total_cells, quarter)
    second_in = normed(inner_cast.astype(jnp.float32)).reshape(frames_dev, HS, W, quarter)
    folded = grid_conv(
        lax.all_gather(second_in, "section", axis=3, tiled=True), w_second, empty_sum
    )
    output = residual.reshape(frames_dev, HS, W, quarter).astype(jnp.float32) + folded
    return output.astype(jnp.bfloat16)


def norm_conv_kernel(split, core_ref, image_ref, mine_ref, other_ref, *rest):
    residual_ref = rest[0] if len(rest) == 4 else None
    out_ref, full_ref, padded_ref = rest[-3:]
    sections, taps, half, quarter = mine_ref.shape
    cells, channels = image_ref.shape[1:]
    group_width = CH // GROUPS

    @pl.when(pl.program_id(0) == 0)
    def _():
        core = core_ref[0]

        @pl.loop(0, taps)
        def _(tap):
            for ref, at in ((mine_ref, core), (other_ref, 1 - core)):
                rows = pl.ds(pl.multiple_of(tap * channels + at * half, half), half)
                for section in range(sections):
                    lanes = slice(section * quarter, (section + 1) * quarter)
                    full_ref[rows, lanes] = ref[section, tap]

        edge = jnp.zeros((W, 3 * channels), jnp.bfloat16)
        padded_ref[:W, :] = edge
        padded_ref[W + cells :, :] = edge

    row_group = lax.div(lax.broadcasted_iota(jnp.int32, (channels, channels), 0), group_width)
    col_group = lax.div(lax.broadcasted_iota(jnp.int32, (channels, channels), 1), group_width)
    same = jnp.where(row_group == col_group, 1.0, 0.0).astype(jnp.float32)

    def group_mean(cellwise):
        per_channel = jnp.sum(cellwise, axis=0, keepdims=True)
        total = jnp.dot(
            jnp.broadcast_to(per_channel, (8, channels)),
            same,
            precision=lax.Precision.HIGHEST,
            preferred_element_type=jnp.float32,
        )
        return total[:1] * (1.0 / (cells * group_width))

    values = image_ref[0].astype(jnp.float32)
    centered = values - group_mean(values)
    scaled = centered * lax.rsqrt(group_mean(centered * centered) + 1e-06)
    active = scaled / (1.0 + jnp.exp(-scaled))
    column = lax.rem(lax.broadcasted_iota(jnp.int32, (cells, channels), 0), W)
    inside = slice(W, W + cells)
    left = jnp.where(column == 0, 0.0, pltpu.roll(active, 1, 0))
    right = jnp.where(column == W - 1, 0.0, pltpu.roll(active, cells - 1, 0))
    padded_ref[inside, :channels] = left.astype(jnp.bfloat16)
    padded_ref[inside, channels : 2 * channels] = active.astype(jnp.bfloat16)
    padded_ref[inside, 2 * channels :] = right.astype(jnp.bfloat16)

    depth = 3 * channels
    width = 2 * quarter
    for block in range(channels // width):
        lanes = slice(block * width, (block + 1) * width)
        total = None
        for row_off in range(3):
            product = jnp.dot(
                padded_ref[row_off * W : row_off * W + cells, :],
                full_ref[row_off * depth : (row_off + 1) * depth, lanes],
                preferred_element_type=jnp.float32,
            )
            total = product if total is None else total + product
        if residual_ref is not None:
            total = total + residual_ref[0, :, lanes].astype(jnp.float32)
        total = total.astype(jnp.bfloat16)
        if split:
            out_ref[0, 2 * block] = total[:, :quarter]
            out_ref[0, 2 * block + 1] = total[:, quarter:]
        else:
            out_ref[0, :, lanes] = total


def norm_conv(image, halves, core, residual=None):
    frames, cells, channels = image.shape
    mine, other = halves
    sections, taps, half, quarter = mine.shape
    split = residual is not None
    frame_spec = pl.BlockSpec((1, cells, channels), lambda i: (i, 0, 0))
    weight_spec = pl.BlockSpec(mine.shape, lambda i: (0, 0, 0, 0))
    in_specs = [pl.BlockSpec(memory_space=pltpu.SMEM), frame_spec, weight_spec, weight_spec]
    operands = [core.reshape(1), image, mine, other]
    out_shape, out_spec = (frames, cells, channels), frame_spec
    if split:
        in_specs.append(frame_spec)
        operands.append(residual)
        out_shape = (frames, sections, cells, quarter)
        out_spec = pl.BlockSpec((1, sections, cells, quarter), lambda i: (i, 0, 0, 0))
    return pl.pallas_call(
        functools.partial(norm_conv_kernel, split),
        grid=(frames,),
        in_specs=in_specs,
        out_specs=out_spec,
        out_shape=jax.ShapeDtypeStruct(out_shape, jnp.bfloat16),
        scratch_shapes=[
            pltpu.VMEM((taps * channels, sections * quarter), jnp.bfloat16),
            pltpu.VMEM((cells + 2 * W, 3 * channels), jnp.bfloat16),
        ],
        compiler_params=pltpu.CompilerParams(vmem_limit_bytes=50 * 1024 * 1024),
        cost_estimate=pl.CostEstimate(
            flops=2 * frames * cells * taps * channels * channels,
            bytes_accessed=2 * taps * channels * channels + 4 * frames * cells * channels,
            transcendentals=frames * cells * channels,
        ),
    )(*operands)


def permute_half(weight, core):
    sections = lax.axis_size("section")
    section_at = lax.axis_index("section")
    half = weight.shape[2] // 2
    own = lax.dynamic_slice_in_dim(weight, core * half, half, 2)
    own = own.reshape((9,) + own.shape[2:])
    parts = [own] + [
        lax.ppermute(own, "section", [(i, i ^ hop) for i in range(sections)])
        for hop in range(1, sections)
    ]
    return jnp.stack(
        [
            lax.select_n(section_at, *[parts[sender ^ s] for s in range(sections)])
            for sender in range(sections)
        ]
    )


def swap_half(mine):
    rows_count = lax.axis_size("rows")
    return mine, lax.ppermute(mine, "rows", [(i, i ^ 1) for i in range(rows_count)])


def unique_frames(latents, w_in, w_time, own):
    size = lax.axis_size("rows")
    row_at = lax.axis_index("rows")
    blocks = [latents] + [
        lax.ppermute(latents, "rows", [(i, (i + hop) % size) for i in range(size)])
        for hop in range(1, size)
    ]
    gathered = jnp.concatenate(
        [
            lax.select_n(row_at, *[blocks[(row - sender) % size] for row in range(size)])
            for sender in range(size)
        ],
        axis=3,
    )
    flat_latents = gathered.reshape(CLIPS * LF, LATC, HS * W)
    clip = own // LF
    at = own % LF
    count = own.shape[0]
    places = jnp.concatenate([jnp.maximum(at - 1, 0), at])
    taps = jnp.maximum(places[:, None] - 2 + jnp.arange(3, dtype=jnp.int32), 0)
    taps = taps + jnp.concatenate([clip, clip])[:, None] * LF
    picked = pick(flat_latents, taps.reshape(-1))
    picked = picked.reshape(2 * count, 3 * LATC, HS * W)
    features = jnp.einsum(
        "nqp,qh->nph", picked, w_in.reshape(3 * LATC, -1), preferred_element_type=jnp.float32
    ).astype(jnp.bfloat16)
    activated = jax.nn.silu(features.astype(jnp.float32)).astype(jnp.bfloat16)
    before, now = activated[:count], activated[count:]
    stacked = jnp.stack(
        [
            jnp.concatenate([before, before, now], axis=2),
            jnp.concatenate([before, now, now], axis=2),
            jnp.concatenate([now, now, now], axis=2),
        ]
    )
    mixed = jnp.einsum(
        "jnpk,kg->jnpg",
        stacked,
        w_time.reshape(-1, w_time.shape[2]),
        preferred_element_type=jnp.float32,
    )
    mixed = mixed + features[count:].astype(jnp.float32)
    return mixed.astype(jnp.bfloat16)


def per_device_frames(latents, w_in, w_time, w_first, w_second):
    sections = lax.axis_size("section")
    rows_count = lax.axis_size("rows")
    section_at = lax.axis_index("section")
    quarter = w_first.shape[3]
    count = CLIPS * LF // rows_count // sections
    first = (lax.axis_index("rows") * sections + section_at) * count
    own = first + jnp.arange(count, dtype=jnp.int32)
    core = lax.axis_index("rows") % 2
    first_halves = swap_half(permute_half(w_first, core))
    second_halves = swap_half(permute_half(w_second, core))
    framed = unique_frames(latents, w_in, w_time, own)
    cells, channels = framed.shape[2:]
    inner = norm_conv(framed.reshape(3 * count, cells, channels), first_halves, core)
    inner = inner.reshape(framed.shape)
    arrived = []
    for frame in range(3):
        out = norm_conv(inner[frame], second_halves, core, framed[frame])
        parts = []
        for hop in range(sections):
            part = lax.dynamic_index_in_dim(out, section_at ^ hop, 1, keepdims=False)
            if hop > 0:
                part = lax.ppermute(part, "section", [(i, i ^ hop) for i in range(sections)])
            parts.append(part)
        arrived.append(parts)
    placed = []
    for sender in range(sections):
        frames = [
            lax.select_n(section_at, *[arrived[f][sender ^ s] for s in range(sections)])
            for f in range(3)
        ]
        placed.append(jnp.stack(frames + [frames[2]], axis=1))
    result = jnp.concatenate(placed, axis=0)
    return result.reshape((sections * count * UPS, HS, W, quarter))


def per_device(latents, w_in, w_time, w_first, w_second):
    sections = lax.axis_size("section")
    rows_count = lax.axis_size("rows")
    even = (CLIPS * LF) % (rows_count * sections) == 0
    if even and rows_count % 2 == 0 and sections > 1 and sections & (sections - 1) == 0:
        return per_device_frames(latents, w_in, w_time, w_first, w_second)
    return per_device_channels(latents, w_in, w_time, w_first, w_second)


def solution(mesh):
    in_specs = (
        P(None, None, None, "rows"),
        P(),
        P(),
        P(None, None, None, "section"),
        P(None, None, None, "section"),
    )
    out_specs = P("rows", None, None, "section")
    return jax.shard_map(
        per_device, mesh=mesh, in_specs=in_specs, out_specs=out_specs, check_vma=False
    )
```
